32 devices in a mesh: dp: 8 (over z, x), vocab: 4 (over y, core).
Axes of the slice: x: 2, y: 2, z: 4, core: 2. Of those that a mesh axis runs over, the one named last changes fastest.
Arguments:
- hidden: bfloat16 [512, 4096], P('dp', 'vocab'), may hold values from -400 to 400
- output_head_matrix: bfloat16 [4096, 151936], P(None, ('dp', 'vocab')), may hold values from -0.09375 to 0.09375
- row_counts: int32 [8], replicated, may hold values from 1 to 64, 256 in all
- token_ids: int32 [256], P('dp'), may hold values from 0 to 151935
- segment_ids: int32 [256], P('dp'), may hold values from 0 to 15, never falling along the last dimension, each value on 1 to 64 neighbouring positions
- cotangent: float32 [256], P('dp'), may hold values from -6 to 6
Outputs:
- logprobs: float32 [256], P('dp')
- grad_hidden: bfloat16 [512, 4096], P('dp', 'vocab')
The draws below stay inside these ranges and needn't reach their ends.
Inputs may be any that keep to these rules, and one draw needn't show every extreme that they name: `row_counts`: live rows of each index of dp; they sum to 256, one index holds 64. `segment_ids`: never falling; each segment has 1 to 64 positions, one exactly 64.
All inputs are finite; a program needn't handle non-finite values.
Results may differ from the reference program's by a relative error of at most 0.0034.
Values may be sent and summed in bfloat16 or wider, within the bound.
A program may use at most 128 MiB of HBM per device.

```python
import math
import jax
import jax.numpy as jnp
import numpy as np
from jax import lax

D = 4096
V = 151936
TOK_DEV = 32
CAP = 64
TOTAL = 256
ROWS_IN = 512
SEGS = 16
SEG_MOST = 64
N_DP = 8
DEVICES = 32


def draw_hidden(key, part):
    key = jax.random.fold_in(key, 7)
    first_key = jax.random.fold_in(key, 0)
    values = jnp.clip(jax.random.normal(first_key, (ROWS_IN, D), jnp.float32), -4.0, 4.0)
    return values.astype(jnp.bfloat16)


def plant(values, key, smallest, high):
    place = [jax.random.randint(jax.random.fold_in(key, axis), (), 0, length) for axis, length in enumerate(values.shape)]
    widest = values.shape.index(max(values.shape))
    neighbour = place[:widest] + [(place[widest] + 1) % values.shape[widest]] + place[widest + 1:]
    return values.at[tuple(place)].set(smallest).at[tuple(neighbour)].set(high)


def block_levels(key, extent, cuts, low, largest):
    factor_of = 1.0
    for axis_at, blocks in cuts:
        draws = jax.random.uniform(jax.random.fold_in(jax.random.fold_in(key, 6), axis_at), (blocks,), jnp.float32, low / len(cuts), largest / len(cuts))
        factor_of = factor_of * jnp.repeat(jnp.exp(draws), extent[axis_at] // blocks).reshape((-1,) + (1,) * (len(extent) - 1 - axis_at))
    return factor_of


def skewed_wide(stream_key, dims, count, skew):
    loads = [min(1 << octave, count + 1 - (1 << octave)) * (1 << 20) // math.isqrt((1 << octave) ** skew) + 1 for octave in range((count + 1).bit_length()) if 1 << octave <= count]
    deviation = 1 + sum(loads) // (1 << 30)
    listing = np.cumsum(np.array([max(1, weight // deviation) for weight in loads]))
    pick = jax.random.randint(jax.random.fold_in(stream_key, 1), dims, 0, int(listing[len(loads) - 1]))
    start = jnp.left_shift(1, jnp.searchsorted(jnp.asarray(listing, jnp.int32), pick, side="right").astype(jnp.int32))
    grade = start - 1 + jax.random.randint(jax.random.fold_in(stream_key, 4), dims, 0, 1 << 30) % jnp.minimum(start, count + 1 - start)
    return jax.random.permutation(jax.random.fold_in(stream_key, 2), count)[grade].astype(jnp.int32)


def split_up(amount, total, limit, skew):
    loads = [(1 << 20) // math.isqrt(standing ** skew) + 1 for standing in range(2, amount + 1)]
    surplus, given = total - limit - (amount - 1), [1] * (amount - 1)
    while surplus > 0:
        free = [i for i in range(amount - 1) if given[i] < limit]
        whole, budget = sum([loads[i] for i in free]), surplus
        for i in free:
            extra = min(limit - given[i], max(1, budget * loads[i] // whole), surplus)
            given[i] = given[i] + extra
            surplus = surplus - extra
    return np.array([limit] + given)


def ragged_sizes(own_key, amount, total, limit, lean):
    if amount == 2:
        one = jax.random.randint(own_key, (), max(1, total - limit), min(limit, total - 1) + 1)
        return jnp.stack([one, total - one])
    tallies = jnp.asarray(split_up(amount, total, limit, lean), jnp.int32)
    couples = (amount - 1) // 2
    source_of, sink = tallies[1:1 + 2 * couples:2], tallies[2:2 + 2 * couples:2]
    margin = jnp.minimum(source_of - 1, limit - sink)
    moved = jax.random.randint(jax.random.fold_in(own_key, 1), (couples,), 0, 1 << 20) % (margin + 1)
    tallies = tallies.at[1:1 + 2 * couples:2].set(source_of - moved).at[2:2 + 2 * couples:2].set(sink + moved)
    return tallies[jax.random.permutation(jax.random.fold_in(own_key, 2), amount)]


def gaussian(own_key, extent, spread, limit, shards=(), kind=jnp.bfloat16):
    entries = spread * jax.random.normal(own_key, extent, jnp.float32)
    if shards:
        entries = entries * block_levels(own_key, extent, shards, -0.22, 0.18)
    return jnp.clip(entries, -limit, limit).astype(kind)


def setup_inputs(seed: int = 0) -> dict:
    keys = jax.random.split(jax.random.key(seed), 7)
    hidden = draw_hidden(jax.random.fold_in(keys[6], 71), 0)
    output_head_matrix = gaussian(keys[1], (D, V), D ** -0.5, 0.09375, ((1, 32),))
    row_counts = ragged_sizes(keys[2], N_DP, TOK_DEV * N_DP, CAP, 2).astype(jnp.int32)
    token_ids = plant(skewed_wide(keys[3], (TOTAL,), V, 2), jax.random.fold_in(keys[3], 3), 0, V - 1).astype(jnp.int32)
    segment_ids = jnp.searchsorted(jnp.cumsum(ragged_sizes(keys[4], SEGS, TOTAL, SEG_MOST, 2)), jnp.arange(TOTAL), side="right").astype(jnp.int32)
    cotangent = gaussian(keys[5], (TOTAL,), 1.0, 6.0, ((0, 8),), jnp.float32)
    return dict(hidden=hidden, output_head_matrix=output_head_matrix, row_counts=row_counts, token_ids=token_ids, segment_ids=segment_ids, cotangent=cotangent)


freq_weight = 0.4
presence_weight = 0.8


def reference(hidden, output_head_matrix, row_counts, token_ids, segment_ids, cotangent):
    ends = jnp.cumsum(row_counts).astype(jnp.int32)
    starts = (ends - row_counts).astype(jnp.int32)
    index = jnp.arange(TOTAL, dtype=jnp.int32)
    rollout = (index % TOK_DEV) * N_DP + index // TOK_DEV
    source = jnp.sum((rollout[:, None] >= ends[None, :]).astype(jnp.int32), axis=1).astype(jnp.int32)
    source_row = (source * CAP + rollout - starts[source]).astype(jnp.int32)
    packed = hidden[source_row]
    prior_token_hits = ((segment_ids[:, None] == segment_ids[None, :]) & (index[None, :] < index[:, None])).astype(jnp.bfloat16)
    block_cols = V // DEVICES

    def forward_block(block):
        first_col = (block * block_cols).astype(jnp.int32)
        weight_cols = lax.dynamic_slice_in_dim(output_head_matrix, first_col, block_cols, 1)
        logits = jnp.dot(packed, weight_cols, preferred_element_type=jnp.float32)
        hits = token_ids[:, None] == first_col + jnp.arange(block_cols, dtype=jnp.int32)[None, :]
        counts = jnp.dot(prior_token_hits, hits.astype(jnp.bfloat16), preferred_element_type=jnp.float32)
        scores = logits - freq_weight * counts - presence_weight * (counts > 0).astype(jnp.float32)
        return scores, jnp.sum(jnp.where(hits, scores, jnp.zeros_like(scores)), axis=1)

    blocks = jnp.arange(DEVICES, dtype=jnp.int32)
    scores, picked = lax.map(forward_block, blocks)
    top = jnp.max(scores, axis=(0, 2))
    total = jnp.sum(jnp.exp(scores - top[None, :, None]), axis=(0, 2))
    logprobs = jnp.sum(picked, axis=0) - top - jnp.log(total)

    def backward_block(summed, inputs):
        block_logit_values, block = inputs
        first_col = (block * block_cols).astype(jnp.int32)
        weight_cols = lax.dynamic_slice_in_dim(output_head_matrix, first_col, block_cols, 1)
        hits = token_ids[:, None] == first_col + jnp.arange(block_cols, dtype=jnp.int32)[None, :]
        residual = (hits.astype(jnp.float32) - jnp.exp(block_logit_values - top[:, None]) / total[:, None]).astype(jnp.bfloat16)
        return summed + jnp.dot(residual, weight_cols.T, preferred_element_type=jnp.float32), None

    summed, _ = lax.scan(backward_block, jnp.zeros((TOTAL, D), jnp.float32), (scores, blocks))
    scaled = (summed * cotangent[:, None]).astype(jnp.bfloat16)
    grad_hidden = jnp.zeros((ROWS_IN, D), jnp.bfloat16).at[source_row].set(scaled)
    return logprobs, grad_hidden
```

```python
import functools

import jax
import jax.numpy as jnp
from jax import lax
from jax.experimental import pallas as pl
from jax.experimental.pallas import tpu as pltpu
from jax.sharding import PartitionSpec as P

freq_weight = 0.4
presence_weight = 0.8
HALVES = 2
BLOCK = 512
MESH = pl.DeviceIdType.MESH


class Grid:
    def __init__(self, dp_count, voc_count):
        z = 4 if dp_count % 4 == 0 else dp_count
        self.size = {"z": z, "x": dp_count // z, "y": voc_count // 2, "c": 2}

    def me(self):
        dp, voc = lax.axis_index("dp"), lax.axis_index("vocab")
        x, c = self.size["x"], self.size["c"]
        return {
            "z": lax.div(dp, x),
            "x": lax.rem(dp, x),
            "y": lax.div(voc, c),
            "c": lax.rem(voc, c),
        }

    def other(self, me, axis, step):
        return lax.rem(me[axis] + step, self.size[axis])

    def device(self, me, axis, at):
        there = dict(me)
        there[axis] = at
        return (
            there["z"] * self.size["x"] + there["x"],
            there["y"] * self.size["c"] + there["c"],
        )

    def barrier(self, me):
        barrier = pltpu.get_barrier_semaphore()
        peers = 0
        for axis in "zxyc":
            for step in range(1, self.size[axis]):
                pl.semaphore_signal(
                    barrier,
                    inc=1,
                    device_id=self.device(me, axis, self.other(me, axis, step)),
                    device_id_type=MESH,
                )
                peers += 1
        pl.semaphore_wait(barrier, peers)


GATHER_ORDERS = ("zxy", "zyx")
SCATTER_ORDERS = ("yxz", "xyz")


def gather_kernel(grid, x_ref, out_ref, send_sem, recv_sem):
    me = grid.me()
    tok_rows, cols = x_ref.shape
    width = cols // HALVES
    for h in range(HALVES):
        out_ref[me["c"], h, me["y"], me["z"], me["x"]] = x_ref[:, h * width : (h + 1) * width]
    grid.barrier(me)
    used = [0]

    def region(h, have, c=None):
        at = [
            pl.ds(0, grid.size[a]) if a in have else pl.ds(have_at(a, h), 1) for a in "yzx"
        ]
        return out_ref.at[me["c"], h, at[0], at[1], at[2]]

    def have_at(a, h):
        return me[a]

    def start(ref, axis, step):
        k = used[0]
        used[0] += 1
        copy = pltpu.make_async_remote_copy(
            src_ref=ref,
            dst_ref=ref,
            send_sem=send_sem.at[k],
            recv_sem=recv_sem.at[k],
            device_id=grid.device(me, axis, grid.other(me, axis, step)),
            device_id_type=MESH,
        )
        copy.start()
        return copy

    core_copies = []
    stages = len(GATHER_ORDERS[0])
    for s in range(stages):
        copies = []
        for h in range(HALVES):
            order = GATHER_ORDERS[h]
            ref = region(h, order[:s])
            for step in range(1, grid.size[order[s]]):
                copies.append(start(ref, order[s], step))
        if s == stages - 1:
            for h in range(HALVES):
                core_copies.append(start(region(h, GATHER_ORDERS[h][:s]), "c", 1))
        for copy in copies:
            copy.wait()
    for h in range(HALVES):
        order = GATHER_ORDERS[h]
        last = order[-1]
        for step in range(1, grid.size[last]):
            at = [
                pl.ds(grid.other(me, a, step), 1) if a == last else pl.ds(0, grid.size[a])
                for a in "yzx"
            ]
            core_copies.append(start(out_ref.at[me["c"], h, at[0], at[1], at[2]], "c", 1))
    for copy in core_copies:
        copy.wait()


def gather_rows(grid, packed):
    tok_rows, cols = packed.shape
    size = grid.size
    n = HALVES * (size["z"] + size["x"] + size["y"] + size["x"] + size["y"])
    shape = (2, HALVES, size["y"], size["z"], size["x"], tok_rows, cols // HALVES)
    out = pl.pallas_call(
        functools.partial(gather_kernel, grid),
        name="gather_rows",
        out_shape=jax.ShapeDtypeStruct(shape, packed.dtype),
        in_specs=[pl.BlockSpec(memory_space=pltpu.VMEM)],
        out_specs=pl.BlockSpec(memory_space=pltpu.VMEM),
        scratch_shapes=[pltpu.SemaphoreType.DMA((n,)), pltpu.SemaphoreType.DMA((n,))],
        compiler_params=pltpu.CompilerParams(
            collective_id=0, has_side_effects=True, vmem_limit_bytes=24 << 20
        ),
    )(packed)
    return out.reshape(shape[:3] + (size["z"] * size["x"] * tok_rows, cols // HALVES))


def stats_kernel(grid, stats_ref, logprob_ref, top_ref, *scratch):
    me = grid.me()
    slots, (send_sem, recv_sem) = dict(zip("yxzc", scratch[:4])), scratch[4:]
    lanes = stats_ref.shape[1]
    held = jnp.transpose(stats_ref[...])[:8]
    top, total, picked = held[0:1], held[1:2], held[2:3]
    grid.barrier(me)
    used = 0
    for axis in "yxzc":
        n = grid.size[axis]
        if n == 1:
            continue
        slot = slots[axis]
        slot[me[axis]] = jnp.concatenate([top, total, picked, jnp.zeros_like(held[3:])], axis=0)
        copies = []
        for step in range(1, n):
            copy = pltpu.make_async_remote_copy(
                src_ref=slot.at[me[axis]],
                dst_ref=slot.at[me[axis]],
                send_sem=send_sem.at[used],
                recv_sem=recv_sem.at[used],
                device_id=grid.device(me, axis, grid.other(me, axis, step)),
                device_id_type=MESH,
            )
            copy.start()
            copies.append(copy)
            used += 1
        for copy in copies:
            copy.wait()
        blocks = [slot[k] for k in range(n)]
        top = functools.reduce(jnp.maximum, [b[0:1] for b in blocks])
        total = sum(b[1:2] * jnp.exp(b[0:1] - top) for b in blocks)
        picked = sum(b[2:3] for b in blocks)
    logprob_ref[...] = jnp.broadcast_to(picked - top - jnp.log(total), logprob_ref.shape)
    rows = top.shape[1]
    both = jnp.concatenate(
        [top, 1.0 / total, jnp.zeros((lanes - 2, rows), jnp.float32)], axis=0
    )
    top_ref[...] = jnp.transpose(both)


def combine_stats(grid, stats):
    rows, lanes = stats.shape
    size = grid.size
    n = sum(size[a] for a in "yxzc")
    vmem = pl.BlockSpec(memory_space=pltpu.VMEM)
    return pl.pallas_call(
        functools.partial(stats_kernel, grid),
        name="combine_stats",
        out_shape=[
            jax.ShapeDtypeStruct((8, rows), jnp.float32),
            jax.ShapeDtypeStruct((rows, lanes), jnp.float32),
        ],
        in_specs=[vmem],
        out_specs=[vmem, vmem],
        scratch_shapes=[pltpu.VMEM((size[a], 8, rows), jnp.float32) for a in "yxzc"]
        + [pltpu.SemaphoreType.DMA((n,)), pltpu.SemaphoreType.DMA((n,))],
        compiler_params=pltpu.CompilerParams(collective_id=1, has_side_effects=True),
    )(stats)


def scatter_kernel(grid, p_ref, out_ref, core_recv, acc, sendbuf, *rest):
    me = grid.me()
    recvs = rest[: HALVES * 3]
    send_sem, recv_sem = rest[HALVES * 3 :]
    used = [0]
    grid.barrier(me)

    def start(src, dst, axis, step):
        k = used[0]
        used[0] += 1
        copy = pltpu.make_async_remote_copy(
            src_ref=src,
            dst_ref=dst,
            send_sem=send_sem.at[k],
            recv_sem=recv_sem.at[k],
            device_id=grid.device(me, axis, grid.other(me, axis, step)),
            device_id_type=MESH,
        )
        copy.start()
        return copy

    there = grid.other(me, "c", 1)
    core = [start(p_ref.at[there, h], core_recv.at[h], "c", 1) for h in range(HALVES)]
    for h in range(HALVES):
        core[h].wait()
        acc[h] = p_ref[me["c"], h] + core_recv[h]

    def cut(h, done, axis, at):
        where = []
        for a in "yzx":
            if a == axis:
                where.append(pl.ds(at, 1))
            elif a in done:
                where.append(pl.ds(me[a], 1))
            else:
                where.append(pl.ds(0, grid.size[a]))
        return (h, where[0], where[1], where[2])

    for s in range(3):
        copies = []
        for h in range(HALVES):
            order = SCATTER_ORDERS[h]
            axis, done = order[s], order[:s]
            recv = recvs[h * 3 + s]
            for step in range(1, grid.size[axis]):
                idx = cut(h, done, axis, grid.other(me, axis, step))
                sendbuf[idx] = acc[idx].astype(sendbuf.dtype)
                copies.append((h, step, start(sendbuf.at[idx], recv.at[step - 1], axis, step)))
        for h, step, copy in copies:
            copy.wait()
            order = SCATTER_ORDERS[h]
            axis, done = order[s], order[:s]
            idx = cut(h, done, axis, me[axis])
            acc[idx] = acc[idx] + recvs[h * 3 + s][step - 1].astype(jnp.float32)
    width = out_ref.shape[1] // HALVES
    for h in range(HALVES):
        out_ref[:, h * width : (h + 1) * width] = acc[h, me["y"], me["z"], me["x"]]


def scatter_sum(grid, product, tok_rows):
    size = grid.size
    width = product.shape[-1]
    part = (HALVES, size["y"], size["z"], size["x"], tok_rows, width)
    product = product.reshape((2,) + part)
    recvs = []
    for h in range(HALVES):
        shape = {a: size[a] for a in "yzx"}
        for axis in SCATTER_ORDERS[h]:
            shape[axis] = 1
            recvs.append(
                pltpu.VMEM(
                    (max(size[axis] - 1, 1),)
                    + tuple(shape[a] for a in "yzx")
                    + (tok_rows, width),
                    jnp.bfloat16,
                )
            )
    n = HALVES * (1 + sum(size[a] for a in "yzx"))
    return pl.pallas_call(
        functools.partial(scatter_kernel, grid),
        name="scatter_sum",
        out_shape=jax.ShapeDtypeStruct((tok_rows, width * HALVES), jnp.float32),
        in_specs=[pl.BlockSpec(memory_space=pltpu.VMEM)],
        out_specs=pl.BlockSpec(memory_space=pltpu.VMEM),
        scratch_shapes=[
            pltpu.VMEM(part, jnp.float32),
            pltpu.VMEM(part, jnp.float32),
            pltpu.VMEM(part, jnp.bfloat16),
        ]
        + recvs
        + [pltpu.SemaphoreType.DMA((n,)), pltpu.SemaphoreType.DMA((n,))],
        compiler_params=pltpu.CompilerParams(
            collective_id=2, has_side_effects=True, vmem_limit_bytes=48 << 20
        ),
    )(product)


def head_rows(grid, c, h, y, width):
    start = (y * grid.size["c"] + c) * HALVES * width + h * width
    return slice(start, start + width)


def pieces(grid):
    return [(c, h, y) for c in range(2) for h in range(HALVES) for y in range(grid.size["y"])]


def forward_kernel(grid, voc_cols, start_ref, x_ref, w_ref, ids_ref, prior_ref, scores_ref, stats_ref):
    j = pl.program_id(0)
    width = x_ref.shape[-1]
    rows = x_ref.shape[-2]
    logits = jnp.zeros((rows, BLOCK), jnp.float32)
    for c, h, y in pieces(grid):
        logits += jnp.dot(
            x_ref[c, h, y],
            w_ref[head_rows(grid, c, h, y, width), :],
            preferred_element_type=jnp.float32,
        )
    column = j * BLOCK + lax.broadcasted_iota(jnp.int32, (rows, BLOCK), 1)
    valid = column < voc_cols
    hits = (ids_ref[...] == column + start_ref[0]) & valid
    counts = jnp.dot(
        prior_ref[...],
        jnp.where(hits, 1.0, 0.0).astype(jnp.bfloat16),
        preferred_element_type=jnp.float32,
    )
    scores = logits - freq_weight * counts - jnp.where(counts > 0, presence_weight, 0.0)
    scores_ref[...] = scores
    picked = jnp.sum(jnp.where(hits, scores, 0.0), axis=1, keepdims=True)
    scores = jnp.where(valid, scores, -jnp.inf)
    lane = lax.broadcasted_iota(jnp.int32, stats_ref.shape, 1)

    @pl.when(j == 0)
    def _():
        stats_ref[...] = jnp.where(lane == 0, -jnp.inf, 0.0)

    old = stats_ref[...]
    top = jnp.maximum(old[:, 0:1], jnp.max(scores, axis=1, keepdims=True))
    total = old[:, 1:2] * jnp.exp(old[:, 0:1] - top) + jnp.sum(
        jnp.exp(scores - top), axis=1, keepdims=True
    )
    stats_ref[...] = jnp.where(
        lane == 0,
        top,
        jnp.where(lane == 1, total, jnp.where(lane == 2, old[:, 2:3] + picked, 0.0)),
    )


def forward(grid, x, head, col_start, ids, prior):
    depth, voc_cols = head.shape
    rows = x.shape[-2]
    blocks = pl.cdiv(voc_cols, BLOCK)
    return pl.pallas_call(
        functools.partial(forward_kernel, grid, voc_cols),
        name="forward_scores",
        grid=(blocks,),
        out_shape=[
            jax.ShapeDtypeStruct((rows, voc_cols), jnp.float32),
            jax.ShapeDtypeStruct((rows, 128), jnp.float32),
        ],
        in_specs=[
            pl.BlockSpec(memory_space=pltpu.SMEM),
            pl.BlockSpec(x.shape, lambda j: (0,) * 5),
            pl.BlockSpec((depth, BLOCK), lambda j: (0, j)),
            pl.BlockSpec((rows, 1), lambda j: (0, 0)),
            pl.BlockSpec((rows, rows), lambda j: (0, 0)),
        ],
        out_specs=[
            pl.BlockSpec((rows, BLOCK), lambda j: (0, j)),
            pl.BlockSpec((rows, 128), lambda j: (0, 0)),
        ],
        compiler_params=pltpu.CompilerParams(vmem_limit_bytes=48 << 20),
        cost_estimate=pl.CostEstimate(
            flops=2 * rows * depth * voc_cols,
            bytes_accessed=2 * depth * voc_cols,
            transcendentals=rows * voc_cols,
        ),
    )(col_start, x, head, ids, prior)


def backward_kernel(grid, voc_cols, start_ref, scores_ref, w_ref, ids_ref, top_ref, out_ref):
    j = pl.program_id(0)
    width = out_ref.shape[-1]
    rows = scores_ref.shape[0]
    column = j * BLOCK + lax.broadcasted_iota(jnp.int32, (rows, BLOCK), 1)
    valid = column < voc_cols
    hits = jnp.where(ids_ref[...] == column + start_ref[0], 1.0, 0.0)
    probs = jnp.exp(scores_ref[...] - top_ref[:, 0:1]) * top_ref[:, 1:2]
    residual = jnp.where(valid, hits - probs, 0.0).astype(jnp.bfloat16)
    last = pl.num_programs(0) - 1
    spare = voc_cols % BLOCK != 0

    def add(masked):
        for c, h, y in pieces(grid):
            w = w_ref[head_rows(grid, c, h, y, width), :]
            if masked:
                inside = lax.broadcasted_iota(jnp.int32, w.shape, 1) < voc_cols % BLOCK
                w = jnp.where(inside, w, jnp.zeros_like(w))
            term = lax.dot_general(
                residual, w, (((1,), (1,)), ((), ())), preferred_element_type=jnp.float32
            )
            out_ref[c, h, y] += term

    @pl.when(j == 0)
    def _():
        out_ref[...] = jnp.zeros_like(out_ref)

    if spare:
        pl.when(j != last)(lambda: add(False))
        pl.when(j == last)(lambda: add(True))
    else:
        add(False)


def backward(grid, scores, head, col_start, ids, tops, shape):
    depth, voc_cols = head.shape
    rows = scores.shape[0]
    return pl.pallas_call(
        functools.partial(backward_kernel, grid, voc_cols),
        name="backward_product",
        grid=(pl.cdiv(voc_cols, BLOCK),),
        out_shape=jax.ShapeDtypeStruct(shape, jnp.float32),
        in_specs=[
            pl.BlockSpec(memory_space=pltpu.SMEM),
            pl.BlockSpec((rows, BLOCK), lambda j: (0, j)),
            pl.BlockSpec((depth, BLOCK), lambda j: (0, j)),
            pl.BlockSpec((rows, 1), lambda j: (0, 0)),
            pl.BlockSpec(tops.shape, lambda j: (0, 0)),
        ],
        out_specs=pl.BlockSpec(shape, lambda j: (0,) * 5),
        compiler_params=pltpu.CompilerParams(vmem_limit_bytes=48 << 20),
        cost_estimate=pl.CostEstimate(
            flops=2 * rows * depth * voc_cols,
            bytes_accessed=2 * depth * voc_cols,
            transcendentals=rows * voc_cols,
        ),
    )(col_start, scores, head, ids, tops)


def per_device(hidden, output_head_matrix, row_counts, token_ids, segment_ids, cotangent):
    dp_count = lax.axis_size("dp")
    voc_count = lax.axis_size("vocab")
    dp_index = lax.axis_index("dp")
    grid = Grid(dp_count, voc_count)
    slot_rows, feat_cols = hidden.shape
    per_peer = slot_rows // dp_count
    tok_rows = token_ids.shape[0]
    total_rows = tok_rows * dp_count
    voc_cols = output_head_matrix.shape[1]
    ends = jnp.cumsum(row_counts)
    starts = ends - row_counts
    my_start = starts[dp_index]
    live = jnp.arange(slot_rows, dtype=jnp.int32) < row_counts[dp_index]
    outgoing = jnp.where(live[:, None], hidden, jnp.zeros_like(hidden))
    outgoing = jnp.roll(outgoing.reshape(per_peer, dp_count, feat_cols), my_start, axis=1)
    arrived = lax.all_to_all(outgoing, "dp", split_axis=1, concat_axis=1, tiled=True)
    offsets = jnp.mod(dp_index - starts, dp_count)
    base_pos = (starts + offsets - dp_index) // dp_count
    turns = jnp.arange(per_peer, dtype=jnp.int32)[:, None]
    valid = turns * dp_count + offsets[None, :] < row_counts[None, :]
    target_position = (base_pos[None, :] + turns).reshape(-1)
    placing = (
        target_position[None, :] == jnp.arange(tok_rows, dtype=jnp.int32)[:, None]
    ) & valid.reshape(-1)[None, :]
    placing = placing.astype(jnp.bfloat16)
    packed = jnp.dot(
        placing, arrived.reshape(per_peer * dp_count, feat_cols), preferred_element_type=jnp.float32
    ).astype(jnp.bfloat16)
    both = lax.all_to_all(
        jnp.broadcast_to(jnp.stack([token_ids, segment_ids])[None], (dp_count, 2, tok_rows)),
        "dp",
        split_axis=0,
        concat_axis=0,
        tiled=True,
    )
    ids_all, segs_all = both[:, 0].reshape(-1), both[:, 1].reshape(-1)
    positions = jnp.arange(total_rows, dtype=jnp.int32)
    prior = (
        (segs_all[:, None] == segs_all[None, :]) & (positions[None, :] < positions[:, None])
    ).astype(jnp.bfloat16)
    x = gather_rows(grid, packed)
    col_start = ((dp_index * voc_count + lax.axis_index("vocab")) * voc_cols).reshape(1)
    ids = ids_all[:, None]
    scores, stats = forward(grid, x, output_head_matrix, col_start, ids, prior)
    all_logprobs, tops = combine_stats(grid, stats)
    logprobs = lax.dynamic_slice_in_dim(all_logprobs[0], dp_index * tok_rows, tok_rows, 0)
    product = backward(grid, scores, output_head_matrix, col_start, ids, tops, x.shape)
    summed = scatter_sum(grid, product, tok_rows)
    scaled = (summed * cotangent[:, None]).astype(jnp.bfloat16)
    sending = jnp.dot(placing.T, scaled, preferred_element_type=jnp.float32).astype(jnp.bfloat16)
    sending = sending.reshape(per_peer, dp_count, feat_cols)
    returned = lax.all_to_all(sending, "dp", split_axis=1, concat_axis=1, tiled=True)
    grad_hidden = jnp.roll(returned, -my_start, axis=1).reshape(slot_rows, feat_cols)
    return (logprobs, grad_hidden)


def solution(mesh):
    return jax.shard_map(
        per_device,
        mesh=mesh,
        in_specs=(P("dp", "vocab"), P(None, ("dp", "vocab")), P(), P("dp"), P("dp"), P("dp")),
        out_specs=(P("dp"), P("dp", "vocab")),
        check_vma=False,
    )
```

```python
import functools

import jax
import jax.numpy as jnp
from jax import lax
from jax.experimental import pallas as pl
from jax.experimental.pallas import tpu as pltpu
from jax.sharding import PartitionSpec as P

freq_weight = 0.4
presence_weight = 0.8
HALVES = 2
BLOCK = 512
MESH = pl.DeviceIdType.MESH


class Grid:
    def __init__(self, dp_count, voc_count):
        z = 4 if dp_count % 4 == 0 else dp_count
        self.size = {"z": z, "x": dp_count // z, "y": voc_count // 2, "c": 2}

    def me(self):
        dp, voc = lax.axis_index("dp"), lax.axis_index("vocab")
        x, c = self.size["x"], self.size["c"]
        return {
            "z": lax.div(dp, x),
            "x": lax.rem(dp, x),
            "y": lax.div(voc, c),
            "c": lax.rem(voc, c),
        }

    def other(self, me, axis, step):
        return lax.rem(me[axis] + step, self.size[axis])

    def device(self, me, axis, at):
        there = dict(me)
        there[axis] = at
        return (
            there["z"] * self.size["x"] + there["x"],
            there["y"] * self.size["c"] + there["c"],
        )

    def groups(self, me):
        dp, voc = lax.axis_index("dp"), lax.axis_index("vocab")
        dp_count = self.size["z"] * self.size["x"]
        voc_count = self.size["y"] * self.size["c"]
        along_dp = [(lax.rem(dp + k, dp_count), voc) for k in range(1, dp_count)]
        along_voc = [(dp, lax.rem(voc + k, voc_count)) for k in range(1, voc_count)]
        return along_dp, along_voc

    def barrier(self, me):
        barrier = pltpu.get_barrier_semaphore()
        along_dp, along_voc = self.groups(me)
        for device in along_dp + along_voc:
            pl.semaphore_signal(barrier, inc=1, device_id=device, device_id_type=MESH)
        pl.semaphore_wait(barrier, len(along_dp) + len(along_voc))


class Sender:
    def __init__(self, send_sem, recv_sem):
        self.send_sem, self.recv_sem, self.used = send_sem, recv_sem, 0

    def start(self, src, dst, device):
        k = self.used
        self.used += 1
        copy = pltpu.make_async_remote_copy(
            src_ref=src,
            dst_ref=dst,
            send_sem=self.send_sem.at[k],
            recv_sem=self.recv_sem.at[k],
            device_id=device,
            device_id_type=MESH,
        )
        copy.start()
        return copy


GATHER_ORDERS = ("zxy", "zyx")
SCATTER_ORDERS = ("yxz", "xyz", "yxz", "xyz")
PARTS = len(SCATTER_ORDERS)


def gather_kernel(
    grid, cols, sent_ref, placing_ref, ids_ref, out_ref, ids_out, arrived, send_sem, recv_sem
):
    me = grid.me()
    dp = lax.axis_index("dp")
    width = cols // HALVES
    sender = Sender(send_sem, recv_sem)
    ids_out[me["z"], me["x"]] = ids_ref[...]
    arrived[dp] = sent_ref[dp]
    grid.barrier(me)
    along_dp, _ = grid.groups(me)
    copies = [sender.start(sent_ref.at[d[0]], arrived.at[dp], d) for d in along_dp]
    id_copies = []

    def send_ids(axis, have):
        at = [pl.ds(0, grid.size[a]) if a in have else pl.ds(me[a], 1) for a in "zx"]
        ref = ids_out.at[at[0], at[1]]
        for step in range(1, grid.size[axis]):
            device = grid.device(me, axis, grid.other(me, axis, step))
            id_copies.append(sender.start(ref, ref, device))

    send_ids("z", "")
    for copy in copies:
        copy.wait()
    blocks, group_rows, group_cols = arrived.shape
    flat = arrived[...].reshape(blocks * group_rows, group_cols)
    packed = jnp.concatenate(
        [
            jnp.dot(placing_ref[g], flat, preferred_element_type=jnp.float32)
            for g in range(cols // group_cols)
        ],
        axis=1,
    ).astype(out_ref.dtype)
    for h in range(HALVES):
        out_ref[me["c"], h, me["y"], me["z"], me["x"]] = packed[:, h * width : (h + 1) * width]

    def start(h, where, axis, step):
        at = [where[a] for a in "yzx"]
        ref = out_ref.at[me["c"], h, at[0], at[1], at[2]]
        return sender.start(ref, ref, grid.device(me, axis, grid.other(me, axis, step)))

    def held(have):
        return {a: pl.ds(0, grid.size[a]) if a in have else pl.ds(me[a], 1) for a in "yzx"}

    stages = len(GATHER_ORDERS[0])
    running = [[] for _ in range(HALVES)]
    core_copies = []
    for s in range(stages + 1):
        for h in range(HALVES):
            order = GATHER_ORDERS[h]
            for copy in running[h]:
                copy.wait()
            if s == stages:
                last = order[-1]
                for step in range(1, grid.size[last]):
                    where = held(order)
                    where[last] = pl.ds(grid.other(me, last, step), 1)
                    core_copies.append(start(h, where, "c", 1))
                continue
            axis, where = order[s], held(order[:s])
            running[h] = [start(h, where, axis, step) for step in range(1, grid.size[axis])]
            if s == stages - 1:
                core_copies.append(start(h, where, "c", 1))
        if s == 0:
            for copy in list(id_copies):
                copy.wait()
            id_copies.clear()
            send_ids("x", "z")
    for copy in id_copies + core_copies:
        copy.wait()


def gather_rows(grid, sent, placing, ids, cols):
    blocks = sent.shape[0]
    tok_rows = placing.shape[1]
    size = grid.size
    n = blocks + size["z"] + size["x"]
    n += HALVES * (size["z"] + size["x"] + size["y"] + size["x"] + size["y"])
    shape = (2, HALVES, size["y"], size["z"], size["x"], tok_rows, cols // HALVES)
    vmem = pl.BlockSpec(memory_space=pltpu.VMEM)
    out, ids_all = pl.pallas_call(
        functools.partial(gather_kernel, grid, cols),
        name="gather_rows",
        out_shape=[
            jax.ShapeDtypeStruct(shape, sent.dtype),
            jax.ShapeDtypeStruct((size["z"], size["x"]) + ids.shape, ids.dtype),
        ],
        in_specs=[vmem] * 3,
        out_specs=[vmem] * 2,
        scratch_shapes=[
            pltpu.VMEM(sent.shape, sent.dtype),
            pltpu.SemaphoreType.DMA((n,)),
            pltpu.SemaphoreType.DMA((n,)),
        ],
        compiler_params=pltpu.CompilerParams(
            collective_id=0, has_side_effects=True, vmem_limit_bytes=24 << 20
        ),
    )(sent, placing, ids)
    return out.reshape(shape[:3] + (blocks * tok_rows, cols // HALVES)), ids_all


def stats_kernel(grid, stats_ref, logprob_ref, top_ref, voc_slots, dp_slots, send_sem, recv_sem):
    me = grid.me()
    along_dp, along_voc = grid.groups(me)
    sender = Sender(send_sem, recv_sem)
    held = stats_ref[...]
    spare = jnp.zeros_like(held[3:])
    grid.barrier(me)
    for slots, at, peers in (
        (voc_slots, lax.axis_index("vocab"), along_voc),
        (dp_slots, lax.axis_index("dp"), along_dp),
    ):
        slots[at] = held
        copies = [sender.start(slots.at[at], slots.at[at], device) for device in peers]
        for copy in copies:
            copy.wait()
        blocks = [slots[k] for k in range(slots.shape[0])]
        top = functools.reduce(jnp.maximum, [b[0:1] for b in blocks])
        total = sum(b[1:2] * jnp.exp(b[0:1] - top) for b in blocks)
        picked = sum(b[2:3] for b in blocks)
        held = jnp.concatenate([top, total, picked, spare], axis=0)
    logprob_ref[...] = jnp.broadcast_to(picked - top - jnp.log(total), logprob_ref.shape)
    top_ref[...] = jnp.concatenate([top, 1.0 / total, picked, spare], axis=0)


def combine_stats(grid, stats):
    size = grid.size
    voc_count, dp_count = size["y"] * size["c"], size["z"] * size["x"]
    n = voc_count + dp_count
    vmem = pl.BlockSpec(memory_space=pltpu.VMEM)
    return pl.pallas_call(
        functools.partial(stats_kernel, grid),
        name="combine_stats",
        out_shape=[jax.ShapeDtypeStruct(stats.shape, jnp.float32)] * 2,
        in_specs=[vmem],
        out_specs=[vmem, vmem],
        scratch_shapes=[
            pltpu.VMEM((voc_count,) + stats.shape, jnp.float32),
            pltpu.VMEM((dp_count,) + stats.shape, jnp.float32),
            pltpu.SemaphoreType.DMA((n,)),
            pltpu.SemaphoreType.DMA((n,)),
        ],
        compiler_params=pltpu.CompilerParams(collective_id=1, has_side_effects=True),
    )(stats)


def scatter_kernel(
    grid, p_ref, cot_ref, placing_ref, out_ref, core_recv, acc, sendbuf, outgoing, *rest
):
    me = grid.me()
    dp = lax.axis_index("dp")
    recvs = rest[: PARTS * 3]
    sender = Sender(*rest[PARTS * 3 :])
    grid.barrier(me)
    there = grid.other(me, "c", 1)
    core = [
        sender.start(p_ref.at[there, h], core_recv.at[h], grid.device(me, "c", there))
        for h in range(PARTS)
    ]

    def cut(h, done, axis, at):
        where = []
        for a in "yzx":
            if a == axis:
                where.append(pl.ds(at, 1))
            elif a in done:
                where.append(pl.ds(me[a], 1))
            else:
                where.append(pl.ds(0, grid.size[a]))
        return (h, where[0], where[1], where[2])

    running = [[] for _ in range(PARTS)]
    for s in range(4):
        for h in range(PARTS):
            order = SCATTER_ORDERS[h]
            if s == 0:
                core[h].wait()
                acc[h] = p_ref[me["c"], h] + core_recv[h]
            else:
                idx = cut(h, order[: s - 1], order[s - 1], me[order[s - 1]])
                for k, copy in enumerate(running[h]):
                    copy.wait()
                    acc[idx] = acc[idx] + recvs[h * 3 + s - 1][k].astype(jnp.float32)
            if s == 3:
                continue
            axis, done = order[s], order[:s]
            running[h] = []
            for step in range(1, grid.size[axis]):
                to = grid.other(me, axis, step)
                idx = cut(h, done, axis, to)
                sendbuf[idx] = acc[idx].astype(sendbuf.dtype)
                running[h].append(
                    sender.start(
                        sendbuf.at[idx], recvs[h * 3 + s].at[step - 1], grid.device(me, axis, to)
                    )
                )
    summed = jnp.concatenate([acc[h, me["y"], me["z"], me["x"]] for h in range(PARTS)], axis=1)
    scaled = (summed * cot_ref[...]).astype(jnp.bfloat16)
    group_cols = outgoing.shape[-1]
    slots = sum(
        jnp.dot(
            placing_ref[g],
            scaled[:, g * group_cols : (g + 1) * group_cols],
            preferred_element_type=jnp.float32,
        )
        for g in range(placing_ref.shape[0])
    )
    outgoing[...] = slots.astype(outgoing.dtype).reshape(outgoing.shape)
    along_dp, _ = grid.groups(me)
    copies = [sender.start(outgoing.at[d[0]], out_ref.at[dp], d) for d in along_dp]
    out_ref[dp] = outgoing[dp]
    for copy in copies:
        copy.wait()


def scatter_sum(grid, product, cotangent, placing, slot_shape):
    size = grid.size
    width = product.shape[-1]
    tok_rows = cotangent.shape[0]
    part = (PARTS, size["y"], size["z"], size["x"], tok_rows, width)
    product = product.reshape((2,) + part)
    recvs = []
    for h in range(PARTS):
        shape = {a: size[a] for a in "yzx"}
        for axis in SCATTER_ORDERS[h]:
            shape[axis] = 1
            recvs.append(
                pltpu.VMEM(
                    (max(size[axis] - 1, 1),)
                    + tuple(shape[a] for a in "yzx")
                    + (tok_rows, width),
                    jnp.bfloat16,
                )
            )
    n = PARTS * (1 + sum(size[a] for a in "yzx")) + slot_shape[0]
    vmem = pl.BlockSpec(memory_space=pltpu.VMEM)
    return pl.pallas_call(
        functools.partial(scatter_kernel, grid),
        name="scatter_sum",
        out_shape=jax.ShapeDtypeStruct(slot_shape, jnp.bfloat16),
        in_specs=[vmem] * 3,
        out_specs=vmem,
        scratch_shapes=[
            pltpu.VMEM(part, jnp.float32),
            pltpu.VMEM(part, jnp.float32),
            pltpu.VMEM(part, jnp.bfloat16),
            pltpu.VMEM(slot_shape, jnp.bfloat16),
        ]
        + recvs
        + [pltpu.SemaphoreType.DMA((n,)), pltpu.SemaphoreType.DMA((n,))],
        compiler_params=pltpu.CompilerParams(
            collective_id=2, has_side_effects=True, vmem_limit_bytes=48 << 20
        ),
    )(product, cotangent[:, None], placing)


def feature_span(grid, parts, c, h, y, width):
    start = (y * grid.size["c"] + c) * parts * width + h * width
    return slice(start, start + width)


def pieces(grid, parts):
    return [(c, h, y) for c in range(2) for h in range(parts) for y in range(grid.size["y"])]


def forward_kernel(
    grid, voc_cols, start_ref, x_ref, w_ref, ids_ref, prior_ref, scores_ref, stats_ref, xt_ref
):
    j = pl.program_id(0)
    width = x_ref.shape[-1]
    rows = x_ref.shape[-2]
    row = lax.broadcasted_iota(jnp.int32, stats_ref.shape, 0)

    @pl.when(j == 0)
    def _():
        stats_ref[...] = jnp.where(row == 0, -jnp.inf, 0.0)
        for c, h, y in pieces(grid, HALVES):
            span = feature_span(grid, HALVES, c, h, y, width)
            xt_ref[span, :] = jnp.transpose(x_ref[c, h, y])

    logits = jnp.dot(w_ref[...], xt_ref[...], preferred_element_type=jnp.float32)
    column = j * BLOCK + lax.broadcasted_iota(jnp.int32, (BLOCK, rows), 0)
    valid = column < voc_cols
    hits = (ids_ref[...] == column + start_ref[0]) & valid
    counts = jnp.dot(
        jnp.where(hits, 1.0, 0.0).astype(jnp.bfloat16),
        prior_ref[...],
        preferred_element_type=jnp.float32,
    )
    scores = logits - freq_weight * counts - jnp.where(counts > 0, presence_weight, 0.0)
    scores_ref[...] = scores
    picked = jnp.sum(jnp.where(hits, scores, 0.0), axis=0, keepdims=True)
    scores = jnp.where(valid, scores, -jnp.inf)
    old = stats_ref[...]
    top = jnp.maximum(old[0:1], jnp.max(scores, axis=0, keepdims=True))
    total = old[1:2] * jnp.exp(old[0:1] - top) + jnp.sum(
        jnp.exp(scores - top), axis=0, keepdims=True
    )
    stats_ref[...] = jnp.concatenate([top, total, old[2:3] + picked, old[3:]], axis=0)


def forward(grid, x, head, col_start, ids, prior):
    voc_cols, depth = head.shape
    rows = x.shape[-2]
    return pl.pallas_call(
        functools.partial(forward_kernel, grid, voc_cols),
        name="forward_scores",
        grid=(pl.cdiv(voc_cols, BLOCK),),
        out_shape=[
            jax.ShapeDtypeStruct((voc_cols, rows), jnp.float32),
            jax.ShapeDtypeStruct((8, rows), jnp.float32),
        ],
        in_specs=[
            pl.BlockSpec(memory_space=pltpu.SMEM),
            pl.BlockSpec(x.shape, lambda j: (0,) * 5),
            pl.BlockSpec((BLOCK, depth), lambda j: (j, 0)),
            pl.BlockSpec((1, rows), lambda j: (0, 0)),
            pl.BlockSpec((rows, rows), lambda j: (0, 0)),
        ],
        out_specs=[
            pl.BlockSpec((BLOCK, rows), lambda j: (j, 0)),
            pl.BlockSpec((8, rows), lambda j: (0, 0)),
        ],
        scratch_shapes=[pltpu.VMEM((depth, rows), x.dtype)],
        compiler_params=pltpu.CompilerParams(vmem_limit_bytes=48 << 20),
        cost_estimate=pl.CostEstimate(
            flops=2 * rows * depth * voc_cols,
            bytes_accessed=2 * depth * voc_cols,
            transcendentals=rows * voc_cols,
        ),
    )(col_start, x, head, ids, prior)


def backward_kernel(grid, voc_cols, start_ref, scores_ref, w_ref, ids_ref, top_ref, out_ref):
    j = pl.program_id(0)
    width = out_ref.shape[-1]
    rows = scores_ref.shape[1]
    column = j * BLOCK + lax.broadcasted_iota(jnp.int32, (BLOCK, rows), 0)
    valid = column < voc_cols
    hits = jnp.where(ids_ref[...] == column + start_ref[0], 1.0, 0.0)
    probs = jnp.exp(scores_ref[...] - top_ref[0:1]) * top_ref[1:2]
    residual = jnp.transpose(jnp.where(valid, hits - probs, 0.0)).astype(jnp.bfloat16)
    last = pl.num_programs(0) - 1
    tail = voc_cols % BLOCK

    def add(masked):
        for c, h, y in pieces(grid, PARTS):
            w = w_ref[:, feature_span(grid, PARTS, c, h, y, width)]
            if masked:
                inside = lax.broadcasted_iota(jnp.int32, w.shape, 0) < tail
                w = jnp.where(inside, w, jnp.zeros_like(w))
            out_ref[c, h, y] += jnp.dot(residual, w, preferred_element_type=jnp.float32)

    @pl.when(j == 0)
    def _():
        out_ref[...] = jnp.zeros_like(out_ref)

    if tail:
        pl.when(j != last)(lambda: add(False))
        pl.when(j == last)(lambda: add(True))
    else:
        add(False)


def backward(grid, scores, head, col_start, ids, tops, shape):
    voc_cols, depth = head.shape
    rows = scores.shape[1]
    return pl.pallas_call(
        functools.partial(backward_kernel, grid, voc_cols),
        name="backward_product",
        grid=(pl.cdiv(voc_cols, BLOCK),),
        out_shape=jax.ShapeDtypeStruct(shape, jnp.float32),
        in_specs=[
            pl.BlockSpec(memory_space=pltpu.SMEM),
            pl.BlockSpec((BLOCK, rows), lambda j: (j, 0)),
            pl.BlockSpec((BLOCK, depth), lambda j: (j, 0)),
            pl.BlockSpec((1, rows), lambda j: (0, 0)),
            pl.BlockSpec(tops.shape, lambda j: (0, 0)),
        ],
        out_specs=pl.BlockSpec(shape, lambda j: (0,) * 5),
        compiler_params=pltpu.CompilerParams(vmem_limit_bytes=48 << 20),
        cost_estimate=pl.CostEstimate(
            flops=2 * rows * depth * voc_cols,
            bytes_accessed=2 * depth * voc_cols,
            transcendentals=rows * voc_cols,
        ),
    )(col_start, scores, head, ids, tops)


def per_device(hidden, output_head_matrix, row_counts, token_ids, segment_ids, cotangent):
    dp_count = lax.axis_size("dp")
    voc_count = lax.axis_size("vocab")
    dp_index = lax.axis_index("dp")
    grid = Grid(dp_count, voc_count)
    slot_rows, feat_cols = hidden.shape
    per_peer = slot_rows // dp_count
    tok_rows = token_ids.shape[0]
    total_rows = tok_rows * dp_count
    voc_cols = output_head_matrix.shape[1]
    groups = max(1, 16 // per_peer)
    group_cols = feat_cols // groups
    ends = jnp.cumsum(row_counts)
    starts = ends - row_counts
    my_start = starts[dp_index]
    live = jnp.arange(slot_rows, dtype=jnp.int32) < row_counts[dp_index]
    outgoing = jnp.where(live[:, None], hidden, jnp.zeros_like(hidden))
    outgoing = jnp.roll(outgoing.reshape(per_peer, dp_count, feat_cols), my_start, axis=1)
    outgoing = outgoing.reshape(per_peer, dp_count, groups, group_cols)
    outgoing = outgoing.transpose(1, 2, 0, 3).reshape(dp_count, groups * per_peer, group_cols)
    offsets = jnp.mod(dp_index - starts, dp_count)
    base_pos = (starts + offsets - dp_index) // dp_count
    turns = jnp.arange(per_peer, dtype=jnp.int32)[None, :]
    valid = turns * dp_count + offsets[:, None] < row_counts[:, None]
    target = jnp.where(valid, base_pos[:, None] + turns, -1)
    group = jnp.arange(groups, dtype=jnp.int32)
    target = jnp.where(
        (group[:, None] == group[None, :])[:, None, :, None], target[None, :, None, :], -1
    ).reshape(groups, dp_count * groups * per_peer)
    tok = jnp.arange(tok_rows, dtype=jnp.int32)
    placing = (target[:, None, :] == tok[None, :, None]).astype(jnp.bfloat16)
    placing_back = (target[:, :, None] == tok[None, None, :]).astype(jnp.bfloat16)
    own_ids = jnp.pad(jnp.stack([token_ids, segment_ids]), ((0, 6), (0, 128 - tok_rows)))
    x, ids_all = gather_rows(grid, outgoing, placing, own_ids, feat_cols)
    ids_all = ids_all.reshape(dp_count, 8, 128)[:, :2, :tok_rows]
    ids, segs = ids_all[:, 0].reshape(-1), ids_all[:, 1].reshape(-1)
    positions = jnp.arange(total_rows, dtype=jnp.int32)
    prior = (
        (segs[:, None] == segs[None, :]) & (positions[:, None] < positions[None, :])
    ).astype(jnp.bfloat16)
    col_start = ((dp_index * voc_count + lax.axis_index("vocab")) * voc_cols).reshape(1)
    ids = ids[None, :]
    head = output_head_matrix.T
    scores, stats = forward(grid, x, head, col_start, ids, prior)
    all_logprobs, tops = combine_stats(grid, stats)
    logprobs = lax.dynamic_slice_in_dim(all_logprobs[0], dp_index * tok_rows, tok_rows, 0)
    shape = (2, PARTS, grid.size["y"], total_rows, feat_cols // PARTS)
    product = backward(grid, scores, head, col_start, ids, tops, shape)
    returned = scatter_sum(grid, product, cotangent, placing_back, outgoing.shape)
    returned = returned.reshape(dp_count, groups, per_peer, group_cols)
    returned = returned.transpose(2, 0, 1, 3).reshape(per_peer, dp_count, feat_cols)
    grad_hidden = jnp.roll(returned, -my_start, axis=1).reshape(slot_rows, feat_cols)
    return (logprobs, grad_hidden)


def solution(mesh):
    return jax.shard_map(
        per_device,
        mesh=mesh,
        in_specs=(P("dp", "vocab"), P(None, ("dp", "vocab")), P(), P("dp"), P("dp"), P("dp")),
        out_specs=(P("dp"), P("dp", "vocab")),
        check_vma=False,
    )
```

```python
import functools

import jax
import jax.numpy as jnp
from jax import lax
from jax.experimental import pallas as pl
from jax.experimental.pallas import tpu as pltpu
from jax.sharding import PartitionSpec as P

freq_weight = 0.4
presence_weight = 0.8
HALVES = 2
BLOCK = 512
MESH = pl.DeviceIdType.MESH


class Grid:
    def __init__(self, dp_count, voc_count):
        z = 4 if dp_count % 4 == 0 else dp_count
        self.size = {"z": z, "x": dp_count // z, "y": voc_count // 2, "c": 2}

    def me(self):
        dp, voc = lax.axis_index("dp"), lax.axis_index("vocab")
        x, c = self.size["x"], self.size["c"]
        return {
            "z": lax.div(dp, x),
            "x": lax.rem(dp, x),
            "y": lax.div(voc, c),
            "c": lax.rem(voc, c),
        }

    def other(self, me, axis, step):
        return lax.rem(me[axis] + step, self.size[axis])

    def device(self, me, axis, at):
        there = dict(me)
        there[axis] = at
        return (
            there["z"] * self.size["x"] + there["x"],
            there["y"] * self.size["c"] + there["c"],
        )

    def groups(self, me):
        dp, voc = lax.axis_index("dp"), lax.axis_index("vocab")
        dp_count = self.size["z"] * self.size["x"]
        voc_count = self.size["y"] * self.size["c"]
        along_dp = [(lax.rem(dp + k, dp_count), voc) for k in range(1, dp_count)]
        along_voc = [(dp, lax.rem(voc + k, voc_count)) for k in range(1, voc_count)]
        return along_dp, along_voc

    def barrier(self, me):
        barrier = pltpu.get_barrier_semaphore()
        along_dp, along_voc = self.groups(me)
        for device in along_dp + along_voc:
            pl.semaphore_signal(barrier, inc=1, device_id=device, device_id_type=MESH)
        pl.semaphore_wait(barrier, len(along_dp) + len(along_voc))


class Sender:
    def __init__(self, send_sem, recv_sem):
        self.send_sem, self.recv_sem, self.used = send_sem, recv_sem, 0

    def start(self, src, dst, device):
        k = self.used
        self.used += 1
        copy = pltpu.make_async_remote_copy(
            src_ref=src,
            dst_ref=dst,
            send_sem=self.send_sem.at[k],
            recv_sem=self.recv_sem.at[k],
            device_id=device,
            device_id_type=MESH,
        )
        copy.start()
        return copy


GATHER_ORDERS = ("zxy", "zyx")
SCATTER_ORDERS = ("yxz", "xyz", "yxz", "xyz")
PARTS = len(SCATTER_ORDERS)


def gather(grid, me, sender, cols, sent_ref, placing_ref, ids_ref, out_ref, ids_out, arrived):
    dp = lax.axis_index("dp")
    width = cols // HALVES
    ids_out[me["z"], me["x"]] = ids_ref[...]
    arrived[dp] = sent_ref[dp]
    grid.barrier(me)
    along_dp, _ = grid.groups(me)
    copies = [sender.start(sent_ref.at[d[0]], arrived.at[dp], d) for d in along_dp]
    id_copies = []

    def send_ids(axis, have):
        at = [pl.ds(0, grid.size[a]) if a in have else pl.ds(me[a], 1) for a in "zx"]
        ref = ids_out.at[at[0], at[1]]
        for step in range(1, grid.size[axis]):
            device = grid.device(me, axis, grid.other(me, axis, step))
            id_copies.append(sender.start(ref, ref, device))

    send_ids("z", "")
    for copy in copies:
        copy.wait()
    blocks, group_rows, group_cols = arrived.shape
    flat = arrived[...].reshape(blocks * group_rows, group_cols)
    packed = jnp.concatenate(
        [
            jnp.dot(placing_ref[g], flat, preferred_element_type=jnp.float32)
            for g in range(cols // group_cols)
        ],
        axis=1,
    ).astype(out_ref.dtype)
    for h in range(HALVES):
        out_ref[me["c"], h, me["y"], me["z"], me["x"]] = packed[:, h * width : (h + 1) * width]

    def start(h, where, axis, step):
        at = [where[a] for a in "yzx"]
        ref = out_ref.at[me["c"], h, at[0], at[1], at[2]]
        return sender.start(ref, ref, grid.device(me, axis, grid.other(me, axis, step)))

    def held(have):
        return {a: pl.ds(0, grid.size[a]) if a in have else pl.ds(me[a], 1) for a in "yzx"}

    stages = len(GATHER_ORDERS[0])
    running = [[] for _ in range(HALVES)]
    core_copies = []
    for s in range(stages + 1):
        for h in range(HALVES):
            order = GATHER_ORDERS[h]
            for copy in running[h]:
                copy.wait()
            if s == stages:
                last = order[-1]
                for step in range(1, grid.size[last]):
                    where = held(order)
                    where[last] = pl.ds(grid.other(me, last, step), 1)
                    core_copies.append(start(h, where, "c", 1))
                continue
            axis, where = order[s], held(order[:s])
            running[h] = [start(h, where, axis, step) for step in range(1, grid.size[axis])]
            if s == stages - 1:
                core_copies.append(start(h, where, "c", 1))
        if s == 0:
            for copy in list(id_copies):
                copy.wait()
            id_copies.clear()
            send_ids("x", "z")
    for copy in id_copies + core_copies:
        copy.wait()


def exchange_stats(grid, sender, held, voc_slots, dp_slots):
    along_dp, along_voc = grid.groups(None)
    for slots, at, peers in (
        (voc_slots, lax.axis_index("vocab"), along_voc),
        (dp_slots, lax.axis_index("dp"), along_dp),
    ):
        slots[at] = held
        copies = [sender.start(slots.at[at], slots.at[at], device) for device in peers]
        for copy in copies:
            copy.wait()
        blocks = [slots[k] for k in range(slots.shape[0])]
        top = functools.reduce(jnp.maximum, [b[0:1] for b in blocks])
        total = sum(b[1:2] * jnp.exp(b[0:1] - top) for b in blocks)
        picked = sum(b[2:3] for b in blocks)
        held = jnp.concatenate([top, total, picked, jnp.zeros_like(held[3:])], axis=0)
    return top, total, picked


def scatter(
    grid, me, sender, core, cot_ref, placing_ref, out_ref, core_recv, acc, sendbuf, outgoing, recvs
):
    dp = lax.axis_index("dp")

    def cut(h, done, axis, at):
        where = []
        for a in "yzx":
            if a == axis:
                where.append(pl.ds(at, 1))
            elif a in done:
                where.append(pl.ds(me[a], 1))
            else:
                where.append(pl.ds(0, grid.size[a]))
        return (h, where[0], where[1], where[2])

    running = [[] for _ in range(PARTS)]
    for s in range(4):
        for h in range(PARTS):
            order = SCATTER_ORDERS[h]
            if s == 0:
                core(h).wait()
                acc[h] = acc[h] + core_recv[h]
            else:
                idx = cut(h, order[: s - 1], order[s - 1], me[order[s - 1]])
                for k, copy in enumerate(running[h]):
                    copy.wait()
                    acc[idx] = acc[idx] + recvs[h * 3 + s - 1][k].astype(jnp.float32)
            if s == 3:
                continue
            axis, done = order[s], order[:s]
            running[h] = []
            for step in range(1, grid.size[axis]):
                to = grid.other(me, axis, step)
                idx = cut(h, done, axis, to)
                sendbuf[idx] = acc[idx].astype(sendbuf.dtype)
                running[h].append(
                    sender.start(
                        sendbuf.at[idx], recvs[h * 3 + s].at[step - 1], grid.device(me, axis, to)
                    )
                )
    summed = jnp.concatenate([acc[h, me["y"], me["z"], me["x"]] for h in range(PARTS)], axis=1)
    scaled = (summed * cot_ref[...]).astype(jnp.bfloat16)
    group_cols = outgoing.shape[-1]
    slots = sum(
        jnp.dot(
            placing_ref[g],
            scaled[:, g * group_cols : (g + 1) * group_cols],
            preferred_element_type=jnp.float32,
        )
        for g in range(placing_ref.shape[0])
    )
    outgoing[...] = slots.astype(outgoing.dtype).reshape(outgoing.shape)
    along_dp, _ = grid.groups(me)
    copies = [sender.start(outgoing.at[d[0]], out_ref.at[dp], d) for d in along_dp]
    out_ref[dp] = outgoing[dp]
    for copy in copies:
        copy.wait()


def feature_span(grid, parts, c, h, y, width):
    start = (y * grid.size["c"] + c) * parts * width + h * width
    return pl.ds(start if isinstance(start, int) else pl.multiple_of(start, width), width)


def head_kernel(
    grid,
    voc_cols,
    head_ref,
    tail_ref,
    sent_ref,
    placing_ref,
    back_ref,
    cot_ref,
    ids_ref,
    logprob_ref,
    out_ref,
    head,
    x,
    xt,
    scores,
    residual,
    product,
    core_recv,
    acc,
    sendbuf,
    arrived,
    outgoing,
    ids_all,
    voc_slots,
    dp_slots,
    load_sem,
    send_sem,
    recv_sem,
    core_send_sem,
    core_recv_sem,
    *recvs,
):
    me = grid.me()
    sender = Sender(send_sem, recv_sem)
    padded, depth = head.shape
    rows = xt.shape[1]
    main = voc_cols // 128 * 128
    full, rest = padded // BLOCK, padded % BLOCK
    loads = []
    for k, start in enumerate(range(0, main, BLOCK)):
        span = pl.ds(start, min(BLOCK, main - start))
        loads.append(pltpu.make_async_copy(head_ref.at[span], head.at[span], load_sem.at[k]))
    if padded > main:
        span = pl.ds(main, padded - main)
        loads.append(pltpu.make_async_copy(tail_ref, head.at[span], load_sem.at[len(loads)]))
    for load in loads:
        load.start()
    cols = depth // (grid.size["y"] * grid.size["c"])
    gather(grid, me, sender, cols, sent_ref, placing_ref, ids_ref, x, ids_all, arrived)

    width = cols // HALVES
    for c in range(2):
        for h in range(HALVES):
            for y in range(grid.size["y"]):
                piece = x[c, h, y].reshape(rows, width)
                xt[feature_span(grid, HALVES, c, h, y, width), :] = jnp.transpose(piece)
    every = sum(
        ids_all[z, k] for z in range(grid.size["z"]) for k in range(grid.size["x"])
    )
    ids = every[0:1]
    segs = jnp.broadcast_to(every[1:2].astype(jnp.float32), (rows, rows))
    earlier = lax.broadcasted_iota(jnp.int32, (rows, rows), 0) < lax.broadcasted_iota(
        jnp.int32, (rows, rows), 1
    )
    prior = jnp.where((segs == jnp.transpose(segs)) & earlier, 1.0, 0.0).astype(jnp.bfloat16)
    col_start = (
        lax.axis_index("dp") * (grid.size["y"] * grid.size["c"]) + lax.axis_index("vocab")
    ) * voc_cols
    for load in loads:
        load.wait()

    def block(start, size):
        return pl.ds(start if isinstance(start, int) else pl.multiple_of(start, BLOCK), size)

    def hits_of(start, size):
        column = start + lax.broadcasted_iota(jnp.int32, (size, rows), 0)
        valid = column < voc_cols
        return valid, (ids == column + col_start) & valid

    def multiply(start, size):
        at = block(start, size)
        scores[at, :] = jnp.dot(head[at, :], xt[...], preferred_element_type=jnp.float32)

    def penalize(start, size, held):
        at = block(start, size)
        valid, hits = hits_of(start, size)
        counts = jnp.dot(
            jnp.where(hits, 1.0, 0.0).astype(jnp.bfloat16),
            prior,
            preferred_element_type=jnp.float32,
        )
        value = (
            scores[at, :] - freq_weight * counts - jnp.where(counts > 0, presence_weight, 0.0)
        )
        scores[at, :] = value
        picked = jnp.sum(jnp.where(hits, value, 0.0), axis=0, keepdims=True)
        value = jnp.where(valid, value, -jnp.inf)
        top = jnp.maximum(held[0:1], jnp.max(value, axis=0, keepdims=True))
        total = held[1:2] * jnp.exp(held[0:1] - top) + jnp.sum(
            jnp.exp(value - top), axis=0, keepdims=True
        )
        return jnp.concatenate([top, total, held[2:3] + picked, held[3:]], axis=0)

    def forward_step(j, held):
        held = penalize((j - 1) * BLOCK, BLOCK, held)
        multiply(j * BLOCK, BLOCK)
        return held

    row = lax.broadcasted_iota(jnp.int32, (8, rows), 0)
    held = jnp.where(row == 0, -jnp.inf, 0.0)
    multiply(0, BLOCK)
    held = lax.fori_loop(1, full, forward_step, held)
    held = penalize((full - 1) * BLOCK, BLOCK, held)
    if rest:
        multiply(full * BLOCK, rest)
        held = penalize(full * BLOCK, rest, held)

    top, total, picked = exchange_stats(grid, sender, held, voc_slots, dp_slots)
    logprob_ref[...] = jnp.broadcast_to(picked - top - jnp.log(total), logprob_ref.shape)
    scale = 1.0 / total

    def residual_step(start, size):
        at = block(start, size)
        valid, hits = hits_of(start, size)
        probs = jnp.exp(scores[at, :] - top) * scale
        value = jnp.where(valid, jnp.where(hits, 1.0, 0.0) - probs, 0.0).astype(jnp.bfloat16)
        residual[:, at] = jnp.transpose(value)

    def residual_loop(j, carry):
        residual_step(j * BLOCK, BLOCK)
        return carry

    lax.fori_loop(0, full, residual_loop, 0)
    if rest:
        residual_step(full * BLOCK, rest)

    part_width = cols // PARTS
    there = grid.other(me, "c", 1)

    def core_copy(h):
        return pltpu.make_async_remote_copy(
            src_ref=product.at[h],
            dst_ref=core_recv.at[h],
            send_sem=core_send_sem.at[h],
            recv_sem=core_recv_sem.at[h],
            device_id=grid.device(me, "c", there),
            device_id_type=MESH,
        )

    def backward_part(h, c, into):
        for y in range(grid.size["y"]):
            span = feature_span(grid, PARTS, c, h, y, part_width)
            term = jnp.dot(residual[...], head[:, span], preferred_element_type=jnp.float32)
            into[h, y] = term.reshape(into.shape[2:])

    def send_part(h, carry):
        backward_part(h, there, product)
        core_copy(h).start()
        return carry

    def keep_part(h, carry):
        backward_part(h, me["c"], acc)
        return carry

    lax.fori_loop(0, PARTS, send_part, 0)
    lax.fori_loop(0, PARTS, keep_part, 0)
    scatter(
        grid,
        me,
        sender,
        core_copy,
        cot_ref,
        back_ref,
        out_ref,
        core_recv,
        acc,
        sendbuf,
        outgoing,
        recvs,
    )


def head_step(grid, head, sent, placing, placing_back, cotangent, ids, total_rows):
    size = grid.size
    voc_cols, depth = head.shape
    dp_count, voc_count = size["z"] * size["x"], size["y"] * size["c"]
    tok_rows = placing.shape[1]
    cols = depth // voc_count
    main = voc_cols // 128 * 128
    padded = -(-voc_cols // 128) * 128
    tail = jnp.pad(head[main:], ((0, main + 128 - voc_cols), (0, 0)))
    x_shape = (2, HALVES, size["y"], size["z"], size["x"], tok_rows, cols // HALVES)
    part = (PARTS, size["y"], size["z"], size["x"], tok_rows, cols // PARTS)
    recvs = []
    for h in range(PARTS):
        shape = {a: size[a] for a in "yzx"}
        for axis in SCATTER_ORDERS[h]:
            shape[axis] = 1
            recvs.append(
                pltpu.VMEM(
                    (max(size[axis] - 1, 1),)
                    + tuple(shape[a] for a in "yzx")
                    + (tok_rows, cols // PARTS),
                    jnp.bfloat16,
                )
            )
    n = 3 * dp_count + voc_count + size["z"] + size["x"]
    n += HALVES * (size["z"] + 2 * size["x"] + 2 * size["y"])
    n += PARTS * sum(size[a] for a in "yzx")
    loads = -(-main // BLOCK) + 1
    vmem = pl.BlockSpec(memory_space=pltpu.VMEM)
    hbm = pl.BlockSpec(memory_space=pl.ANY)
    dma = pltpu.SemaphoreType.DMA
    return pl.pallas_call(
        functools.partial(head_kernel, grid, voc_cols),
        name="head_step",
        out_shape=[
            jax.ShapeDtypeStruct((8, total_rows), jnp.float32),
            jax.ShapeDtypeStruct(sent.shape, jnp.bfloat16),
        ],
        in_specs=[hbm, hbm] + [vmem] * 5,
        out_specs=[vmem, vmem],
        scratch_shapes=[
            pltpu.VMEM((padded, depth), jnp.bfloat16),
            pltpu.VMEM(x_shape, jnp.bfloat16),
            pltpu.VMEM((depth, total_rows), jnp.bfloat16),
            pltpu.VMEM((padded, total_rows), jnp.float32),
            pltpu.VMEM((total_rows, padded), jnp.bfloat16),
            pltpu.VMEM(part, jnp.float32),
            pltpu.VMEM(part, jnp.float32),
            pltpu.VMEM(part, jnp.float32),
            pltpu.VMEM(part, jnp.bfloat16),
            pltpu.VMEM(sent.shape, jnp.bfloat16),
            pltpu.VMEM(sent.shape, jnp.bfloat16),
            pltpu.VMEM((size["z"], size["x"]) + ids.shape, ids.dtype),
            pltpu.VMEM((voc_count, 8, total_rows), jnp.float32),
            pltpu.VMEM((dp_count, 8, total_rows), jnp.float32),
            dma((loads,)),
            dma((n,)),
            dma((n,)),
            dma((PARTS,)),
            dma((PARTS,)),
        ]
        + recvs,
        compiler_params=pltpu.CompilerParams(
            collective_id=0, has_side_effects=True, vmem_limit_bytes=62 << 20
        ),
        cost_estimate=pl.CostEstimate(
            flops=4 * total_rows * depth * voc_cols,
            bytes_accessed=2 * depth * voc_cols,
            transcendentals=2 * total_rows * voc_cols,
        ),
    )(head, tail, sent, placing, placing_back, cotangent[:, None], ids)


def per_device(hidden, output_head_matrix, row_counts, token_ids, segment_ids, cotangent):
    dp_count = lax.axis_size("dp")
    voc_count = lax.axis_size("vocab")
    dp_index = lax.axis_index("dp")
    grid = Grid(dp_count, voc_count)
    slot_rows, feat_cols = hidden.shape
    per_peer = slot_rows // dp_count
    tok_rows = token_ids.shape[0]
    total_rows = tok_rows * dp_count
    voc_cols = output_head_matrix.shape[1]
    groups = max(1, 16 // per_peer)
    group_cols = feat_cols // groups
    ends = jnp.cumsum(row_counts)
    starts = ends - row_counts
    my_start = starts[dp_index]
    live = jnp.arange(slot_rows, dtype=jnp.int32) < row_counts[dp_index]
    outgoing = jnp.where(live[:, None], hidden, jnp.zeros_like(hidden))
    outgoing = jnp.roll(outgoing.reshape(per_peer, dp_count, feat_cols), my_start, axis=1)
    outgoing = outgoing.reshape(per_peer, dp_count, groups, group_cols)
    outgoing = outgoing.transpose(1, 2, 0, 3).reshape(dp_count, groups * per_peer, group_cols)
    offsets = jnp.mod(dp_index - starts, dp_count)
    base_pos = (starts + offsets - dp_index) // dp_count
    turns = jnp.arange(per_peer, dtype=jnp.int32)[None, :]
    valid = turns * dp_count + offsets[:, None] < row_counts[:, None]
    target = jnp.where(valid, base_pos[:, None] + turns, -1)
    group = jnp.arange(groups, dtype=jnp.int32)
    target = jnp.where(
        (group[:, None] == group[None, :])[:, None, :, None], target[None, :, None, :], -1
    ).reshape(groups, dp_count * groups * per_peer)
    tok = jnp.arange(tok_rows, dtype=jnp.int32)
    placing = (target[:, None, :] == tok[None, :, None]).astype(jnp.bfloat16)
    placing_back = (target[:, :, None] == tok[None, None, :]).astype(jnp.bfloat16)
    own_ids = lax.dynamic_update_slice(
        jnp.zeros((8, total_rows), jnp.int32),
        jnp.stack([token_ids, segment_ids]),
        (0, dp_index * tok_rows),
    )
    all_logprobs, returned = head_step(
        grid, output_head_matrix.T, outgoing, placing, placing_back, cotangent, own_ids, total_rows
    )
    logprobs = lax.dynamic_slice_in_dim(all_logprobs[0], dp_index * tok_rows, tok_rows, 0)
    returned = returned.reshape(dp_count, groups, per_peer, group_cols)
    returned = returned.transpose(2, 0, 1, 3).reshape(per_peer, dp_count, feat_cols)
    grad_hidden = jnp.roll(returned, -my_start, axis=1).reshape(slot_rows, feat_cols)
    return (logprobs, grad_hidden)


def solution(mesh):
    return jax.shard_map(
        per_device,
        mesh=mesh,
        in_specs=(P("dp", "vocab"), P(None, ("dp", "vocab")), P(), P("dp"), P("dp"), P("dp")),
        out_specs=(P("dp"), P("dp", "vocab")),
        check_vma=False,
    )
```

```python
import functools

import jax
import jax.numpy as jnp
from jax import lax
from jax.experimental import pallas as pl
from jax.experimental.pallas import tpu as pltpu
from jax.sharding import PartitionSpec as P

freq_weight = 0.4
presence_weight = 0.8
HALVES = 2
BLOCK = 512
MESH = pl.DeviceIdType.MESH


class Grid:
    def __init__(self, dp_count, voc_count):
        z = 4 if dp_count % 4 == 0 else dp_count
        self.size = {"z": z, "x": dp_count // z, "y": voc_count // 2, "c": 2}

    def me(self):
        dp, voc = lax.axis_index("dp"), lax.axis_index("vocab")
        x, c = self.size["x"], self.size["c"]
        return {
            "z": lax.div(dp, x),
            "x": lax.rem(dp, x),
            "y": lax.div(voc, c),
            "c": lax.rem(voc, c),
        }

    def other(self, me, axis, step):
        return lax.rem(me[axis] + step, self.size[axis])

    def device(self, me, axis, at):
        there = dict(me)
        there[axis] = at
        return (
            there["z"] * self.size["x"] + there["x"],
            there["y"] * self.size["c"] + there["c"],
        )

    def groups(self, me):
        dp, voc = lax.axis_index("dp"), lax.axis_index("vocab")
        dp_count = self.size["z"] * self.size["x"]
        voc_count = self.size["y"] * self.size["c"]
        along_dp = [(lax.rem(dp + k, dp_count), voc) for k in range(1, dp_count)]
        along_voc = [(dp, lax.rem(voc + k, voc_count)) for k in range(1, voc_count)]
        return along_dp, along_voc

    def barrier(self, me):
        barrier = pltpu.get_barrier_semaphore()
        along_dp, along_voc = self.groups(me)
        for device in along_dp + along_voc:
            pl.semaphore_signal(barrier, inc=1, device_id=device, device_id_type=MESH)
        pl.semaphore_wait(barrier, len(along_dp) + len(along_voc))


class Sender:
    def __init__(self, send_sem, recv_sem):
        self.send_sem, self.recv_sem, self.used = send_sem, recv_sem, 0

    def start(self, src, dst, device):
        k = self.used
        self.used += 1
        copy = pltpu.make_async_remote_copy(
            src_ref=src,
            dst_ref=dst,
            send_sem=self.send_sem.at[k],
            recv_sem=self.recv_sem.at[k],
            device_id=device,
            device_id_type=MESH,
        )
        copy.start()
        return copy


GATHER_ORDERS = ("zxy", "zyx")
SCATTER_ORDERS = ("yxz", "xyz", "yxz", "xyz")
PARTS = len(SCATTER_ORDERS)


def gather(grid, me, sender, cols, sent_ref, placing_ref, ids_ref, out_ref, ids_out, arrived):
    dp = lax.axis_index("dp")
    width = cols // HALVES
    ids_out[me["z"], me["x"]] = ids_ref[...]
    arrived[dp] = sent_ref[dp]
    grid.barrier(me)
    along_dp, _ = grid.groups(me)
    copies = [sender.start(sent_ref.at[d[0]], arrived.at[dp], d) for d in along_dp]
    id_copies = []

    def send_ids(axis, have):
        at = [pl.ds(0, grid.size[a]) if a in have else pl.ds(me[a], 1) for a in "zx"]
        ref = ids_out.at[at[0], at[1]]
        for step in range(1, grid.size[axis]):
            device = grid.device(me, axis, grid.other(me, axis, step))
            id_copies.append(sender.start(ref, ref, device))

    send_ids("z", "")
    for copy in copies:
        copy.wait()
    blocks, group_rows, group_cols = arrived.shape
    flat = arrived[...].reshape(blocks * group_rows, group_cols)
    packed = jnp.concatenate(
        [
            jnp.dot(placing_ref[g], flat, preferred_element_type=jnp.float32)
            for g in range(cols // group_cols)
        ],
        axis=1,
    ).astype(out_ref.dtype)
    for h in range(HALVES):
        out_ref[me["c"], h, me["y"], me["z"], me["x"]] = packed[:, h * width : (h + 1) * width]

    def start(h, where, axis, step):
        at = [where[a] for a in "yzx"]
        ref = out_ref.at[me["c"], h, at[0], at[1], at[2]]
        return sender.start(ref, ref, grid.device(me, axis, grid.other(me, axis, step)))

    def held(have):
        return {a: pl.ds(0, grid.size[a]) if a in have else pl.ds(me[a], 1) for a in "yzx"}

    stages = len(GATHER_ORDERS[0])
    running = [[] for _ in range(HALVES)]
    core_copies = []
    for s in range(stages + 1):
        for h in range(HALVES):
            order = GATHER_ORDERS[h]
            for copy in running[h]:
                copy.wait()
            if s == stages:
                last = order[-1]
                for step in range(1, grid.size[last]):
                    where = held(order)
                    where[last] = pl.ds(grid.other(me, last, step), 1)
                    core_copies.append(start(h, where, "c", 1))
                continue
            axis, where = order[s], held(order[:s])
            running[h] = [start(h, where, axis, step) for step in range(1, grid.size[axis])]
            if s == stages - 1:
                core_copies.append(start(h, where, "c", 1))
        if s == 0:
            for copy in list(id_copies):
                copy.wait()
            id_copies.clear()
            send_ids("x", "z")
    for copy in id_copies + core_copies:
        copy.wait()


def exchange_stats(grid, sender, held, voc_slots, dp_slots):
    along_dp, along_voc = grid.groups(None)
    for slots, at, peers in (
        (voc_slots, lax.axis_index("vocab"), along_voc),
        (dp_slots, lax.axis_index("dp"), along_dp),
    ):
        slots[at] = held
        copies = [sender.start(slots.at[at], slots.at[at], device) for device in peers]
        for copy in copies:
            copy.wait()
        blocks = [slots[k] for k in range(slots.shape[0])]
        top = functools.reduce(jnp.maximum, [b[0:1] for b in blocks])
        total = sum(b[1:2] * jnp.exp(b[0:1] - top) for b in blocks)
        picked = sum(b[2:3] for b in blocks)
        held = jnp.concatenate([top, total, picked, jnp.zeros_like(held[3:])], axis=0)
    return top, total, picked


def scatter(
    grid, me, sender, keep_part, core, cot_ref, placing_ref, out_ref, core_recv, acc, sendbuf, outgoing, recvs
):
    dp = lax.axis_index("dp")

    def cut(h, done, axis, at):
        where = []
        for a in "yzx":
            if a == axis:
                where.append(pl.ds(at, 1))
            elif a in done:
                where.append(pl.ds(me[a], 1))
            else:
                where.append(pl.ds(0, grid.size[a]))
        return (h, where[0], where[1], where[2])

    running = [[] for _ in range(PARTS)]
    for s in range(4):
        for h in range(PARTS):
            order = SCATTER_ORDERS[h]
            if s == 0:
                keep_part(h)
                core(h).wait()
                acc[h] = acc[h] + core_recv[h]
            else:
                idx = cut(h, order[: s - 1], order[s - 1], me[order[s - 1]])
                for k, copy in enumerate(running[h]):
                    copy.wait()
                    acc[idx] = acc[idx] + recvs[h * 3 + s - 1][k].astype(jnp.float32)
            if s == 3:
                continue
            axis, done = order[s], order[:s]
            running[h] = []
            for step in range(1, grid.size[axis]):
                to = grid.other(me, axis, step)
                idx = cut(h, done, axis, to)
                sendbuf[idx] = acc[idx].astype(sendbuf.dtype)
                running[h].append(
                    sender.start(
                        sendbuf.at[idx], recvs[h * 3 + s].at[step - 1], grid.device(me, axis, to)
                    )
                )
    summed = jnp.concatenate([acc[h, me["y"], me["z"], me["x"]] for h in range(PARTS)], axis=1)
    scaled = (summed * cot_ref[:, 0:1]).astype(jnp.bfloat16)
    group_cols = outgoing.shape[-1]
    slots = sum(
        jnp.dot(
            placing_ref[g],
            scaled[:, g * group_cols : (g + 1) * group_cols],
            preferred_element_type=jnp.float32,
        )
        for g in range(placing_ref.shape[0])
    )
    outgoing[...] = slots.astype(outgoing.dtype).reshape(outgoing.shape)
    along_dp, _ = grid.groups(me)
    copies = [sender.start(outgoing.at[d[0]], out_ref.at[dp], d) for d in along_dp]
    out_ref[dp] = outgoing[dp]
    for copy in copies:
        copy.wait()


def feature_span(grid, parts, c, h, y, width):
    start = (y * grid.size["c"] + c) * parts * width + h * width
    return pl.ds(start if isinstance(start, int) else pl.multiple_of(start, width), width)


def head_kernel(
    grid,
    voc_cols,
    head_ref,
    tail_ref,
    sent_ref,
    placing_ref,
    back_ref,
    cot_ref,
    ids_ref,
    logprob_ref,
    out_ref,
    head,
    x,
    xt,
    scores,
    residual,
    product,
    core_recv,
    acc,
    sendbuf,
    arrived,
    outgoing,
    ids_all,
    voc_slots,
    dp_slots,
    load_sem,
    send_sem,
    recv_sem,
    core_send_sem,
    core_recv_sem,
    *recvs,
):
    me = grid.me()
    sender = Sender(send_sem, recv_sem)
    padded, depth = head.shape
    rows = xt.shape[1]
    main = voc_cols // 128 * 128
    full, rest = padded // BLOCK, padded % BLOCK
    loads = []
    for k, start in enumerate(range(0, main, BLOCK)):
        span = pl.ds(start, min(BLOCK, main - start))
        loads.append(pltpu.make_async_copy(head_ref.at[span], head.at[span], load_sem.at[k]))
    if padded > main:
        span = pl.ds(main, padded - main)
        loads.append(pltpu.make_async_copy(tail_ref, head.at[span], load_sem.at[len(loads)]))
    for load in loads:
        load.start()
    cols = depth // (grid.size["y"] * grid.size["c"])
    gather(grid, me, sender, cols, sent_ref, placing_ref, ids_ref, x, ids_all, arrived)

    width = cols // HALVES
    for c in range(2):
        for h in range(HALVES):
            for y in range(grid.size["y"]):
                piece = x[c, h, y].reshape(rows, width)
                xt[feature_span(grid, HALVES, c, h, y, width), :] = jnp.transpose(piece)
    every = sum(
        ids_all[z, k] for z in range(grid.size["z"]) for k in range(grid.size["x"])
    )
    ids = every[0:1]
    segs = jnp.broadcast_to(every[1:2].astype(jnp.float32), (rows, rows))
    earlier = lax.broadcasted_iota(jnp.int32, (rows, rows), 0) < lax.broadcasted_iota(
        jnp.int32, (rows, rows), 1
    )
    prior = jnp.where((segs == jnp.transpose(segs)) & earlier, 1.0, 0.0).astype(jnp.bfloat16)
    col_start = (
        lax.axis_index("dp") * (grid.size["y"] * grid.size["c"]) + lax.axis_index("vocab")
    ) * voc_cols
    for load in loads:
        load.wait()

    def block(start, size):
        return pl.ds(start if isinstance(start, int) else pl.multiple_of(start, BLOCK), size)

    def hits_of(start, size):
        column = start + lax.broadcasted_iota(jnp.int32, (size, rows), 0)
        valid = column < voc_cols
        return valid, (ids == column + col_start) & valid

    def multiply(start, size):
        at = block(start, size)
        scores[at, :] = jnp.dot(head[at, :], xt[...], preferred_element_type=jnp.float32)

    def penalize(start, size, held):
        at = block(start, size)
        valid, hits = hits_of(start, size)
        counts = jnp.dot(
            jnp.where(hits, 1.0, 0.0).astype(jnp.bfloat16),
            prior,
            preferred_element_type=jnp.float32,
        )
        value = (
            scores[at, :] - freq_weight * counts - jnp.where(counts > 0, presence_weight, 0.0)
        )
        scores[at, :] = value
        picked = jnp.sum(jnp.where(hits, value, 0.0), axis=0, keepdims=True)
        value = jnp.where(valid, value, -jnp.inf)
        top = jnp.maximum(held[0:1], jnp.max(value, axis=0, keepdims=True))
        total = held[1:2] * jnp.exp(held[0:1] - top) + jnp.sum(
            jnp.exp(value - top), axis=0, keepdims=True
        )
        return jnp.concatenate([top, total, held[2:3] + picked, held[3:]], axis=0)

    def forward_step(j, held):
        held = penalize((j - 1) * BLOCK, BLOCK, held)
        multiply(j * BLOCK, BLOCK)
        return held

    row = lax.broadcasted_iota(jnp.int32, (8, rows), 0)
    held = jnp.where(row == 0, -jnp.inf, 0.0)
    multiply(0, BLOCK)
    held = lax.fori_loop(1, full, forward_step, held)
    held = penalize((full - 1) * BLOCK, BLOCK, held)
    if rest:
        multiply(full * BLOCK, rest)
        held = penalize(full * BLOCK, rest, held)

    top, total, picked = exchange_stats(grid, sender, held, voc_slots, dp_slots)
    logprob_ref[...] = jnp.broadcast_to(picked - top - jnp.log(total), logprob_ref.shape)
    scale = 1.0 / total

    def residual_step(start, size):
        at = block(start, size)
        valid, hits = hits_of(start, size)
        probs = jnp.exp(scores[at, :] - top) * scale
        value = jnp.where(valid, jnp.where(hits, 1.0, 0.0) - probs, 0.0).astype(jnp.bfloat16)
        residual[:, at] = jnp.transpose(value)

    def residual_loop(j, carry):
        residual_step(j * BLOCK, BLOCK)
        return carry

    lax.fori_loop(0, full, residual_loop, 0)
    if rest:
        residual_step(full * BLOCK, rest)

    part_width = cols // PARTS
    there = grid.other(me, "c", 1)

    def core_copy(h):
        return pltpu.make_async_remote_copy(
            src_ref=product.at[h],
            dst_ref=core_recv.at[h],
            send_sem=core_send_sem.at[h],
            recv_sem=core_recv_sem.at[h],
            device_id=grid.device(me, "c", there),
            device_id_type=MESH,
        )

    def backward_part(h, c, into):
        for y in range(grid.size["y"]):
            span = feature_span(grid, PARTS, c, h, y, part_width)
            term = jnp.dot(residual[...], head[:, span], preferred_element_type=jnp.float32)
            into[h, y] = term.reshape(into.shape[2:])

    def send_part(h, carry):
        backward_part(h, there, product)
        core_copy(h).start()
        return carry

    def keep_part(h):
        backward_part(h, me["c"], acc)

    lax.fori_loop(0, PARTS, send_part, 0)
    scatter(
        grid,
        me,
        sender,
        keep_part,
        core_copy,
        cot_ref,
        back_ref,
        out_ref,
        core_recv,
        acc,
        sendbuf,
        outgoing,
        recvs,
    )


def head_step(grid, head, sent, placing, placing_back, cotangent, ids, total_rows):
    size = grid.size
    voc_cols, depth = head.shape
    dp_count, voc_count = size["z"] * size["x"], size["y"] * size["c"]
    tok_rows = placing.shape[1]
    cols = depth // voc_count
    main = voc_cols // 128 * 128
    padded = -(-voc_cols // 128) * 128
    tail = jnp.pad(head[main:], ((0, main + 128 - voc_cols), (0, 0)))
    x_shape = (2, HALVES, size["y"], size["z"], size["x"], tok_rows, cols // HALVES)
    part = (PARTS, size["y"], size["z"], size["x"], tok_rows, cols // PARTS)
    recvs = []
    for h in range(PARTS):
        shape = {a: size[a] for a in "yzx"}
        for axis in SCATTER_ORDERS[h]:
            shape[axis] = 1
            recvs.append(
                pltpu.VMEM(
                    (max(size[axis] - 1, 1),)
                    + tuple(shape[a] for a in "yzx")
                    + (tok_rows, cols // PARTS),
                    jnp.bfloat16,
                )
            )
    n = 3 * dp_count + voc_count + size["z"] + size["x"]
    n += HALVES * (size["z"] + 2 * size["x"] + 2 * size["y"])
    n += PARTS * sum(size[a] for a in "yzx")
    loads = -(-main // BLOCK) + 1
    vmem = pl.BlockSpec(memory_space=pltpu.VMEM)
    hbm = pl.BlockSpec(memory_space=pl.ANY)
    dma = pltpu.SemaphoreType.DMA
    return pl.pallas_call(
        functools.partial(head_kernel, grid, voc_cols),
        name="head_step",
        out_shape=[
            jax.ShapeDtypeStruct((8, total_rows), jnp.float32),
            jax.ShapeDtypeStruct(sent.shape, jnp.bfloat16),
        ],
        in_specs=[hbm, hbm] + [vmem] * 5,
        out_specs=[vmem, vmem],
        scratch_shapes=[
            pltpu.VMEM((padded, depth), jnp.bfloat16),
            pltpu.VMEM(x_shape, jnp.bfloat16),
            pltpu.VMEM((depth, total_rows), jnp.bfloat16),
            pltpu.VMEM((padded, total_rows), jnp.float32),
            pltpu.VMEM((total_rows, padded), jnp.bfloat16),
            pltpu.VMEM(part, jnp.float32),
            pltpu.VMEM(part, jnp.float32),
            pltpu.VMEM(part, jnp.float32),
            pltpu.VMEM(part, jnp.bfloat16),
            pltpu.VMEM(sent.shape, jnp.bfloat16),
            pltpu.VMEM(sent.shape, jnp.bfloat16),
            pltpu.VMEM((size["z"], size["x"]) + ids.shape, ids.dtype),
            pltpu.VMEM((voc_count, 8, total_rows), jnp.float32),
            pltpu.VMEM((dp_count, 8, total_rows), jnp.float32),
            dma((loads,)),
            dma((n,)),
            dma((n,)),
            dma((PARTS,)),
            dma((PARTS,)),
        ]
        + recvs,
        compiler_params=pltpu.CompilerParams(
            collective_id=0, has_side_effects=True, vmem_limit_bytes=62 << 20
        ),
        cost_estimate=pl.CostEstimate(
            flops=4 * total_rows * depth * voc_cols,
            bytes_accessed=2 * depth * voc_cols,
            transcendentals=2 * total_rows * voc_cols,
        ),
    )(head, tail, sent, placing, placing_back, jnp.broadcast_to(cotangent[:, None], (tok_rows, 128)), ids)


def per_device(hidden, output_head_matrix, row_counts, token_ids, segment_ids, cotangent):
    dp_count = lax.axis_size("dp")
    voc_count = lax.axis_size("vocab")
    dp_index = lax.axis_index("dp")
    grid = Grid(dp_count, voc_count)
    slot_rows, feat_cols = hidden.shape
    per_peer = slot_rows // dp_count
    tok_rows = token_ids.shape[0]
    total_rows = tok_rows * dp_count
    voc_cols = output_head_matrix.shape[1]
    groups = max(1, 16 // per_peer)
    group_cols = feat_cols // groups
    device = jnp.arange(dp_count, dtype=jnp.int32)
    starts = jnp.sum(jnp.where(device[None, :] < device[:, None], row_counts[None, :], 0), axis=1)
    my_start = jnp.sum(jnp.where(device < dp_index, row_counts, 0))
    my_count = jnp.sum(jnp.where(device == dp_index, row_counts, 0))
    live = jnp.arange(slot_rows, dtype=jnp.int32) < my_count
    outgoing = jnp.where(live[:, None], hidden, jnp.zeros_like(hidden))
    outgoing = jnp.roll(outgoing.reshape(per_peer, dp_count, feat_cols), my_start, axis=1)
    outgoing = outgoing.reshape(per_peer, dp_count, groups, group_cols)
    outgoing = outgoing.transpose(1, 2, 0, 3).reshape(dp_count, groups * per_peer, group_cols)
    offsets = jnp.mod(dp_index - starts, dp_count)
    base_pos = (starts + offsets - dp_index) // dp_count
    turns = jnp.arange(per_peer, dtype=jnp.int32)[None, :]
    valid = turns * dp_count + offsets[:, None] < row_counts[:, None]
    target = jnp.where(valid, base_pos[:, None] + turns, -1)
    group = jnp.arange(groups, dtype=jnp.int32)
    target = jnp.where(
        (group[:, None] == group[None, :])[:, None, :, None], target[None, :, None, :], -1
    ).reshape(groups, dp_count * groups * per_peer)
    tok = jnp.arange(tok_rows, dtype=jnp.int32)
    placing = (target[:, None, :] == tok[None, :, None]).astype(jnp.bfloat16)
    placing_back = (target[:, :, None] == tok[None, None, :]).astype(jnp.bfloat16)
    own_ids = lax.dynamic_update_slice(
        jnp.zeros((8, total_rows), jnp.int32),
        jnp.stack([token_ids, segment_ids]),
        (0, dp_index * tok_rows),
    )
    all_logprobs, returned = head_step(
        grid, output_head_matrix.T, outgoing, placing, placing_back, cotangent, own_ids, total_rows
    )
    logprobs = lax.dynamic_slice_in_dim(all_logprobs[0], dp_index * tok_rows, tok_rows, 0)
    returned = returned.reshape(dp_count, groups, per_peer, group_cols)
    returned = returned.transpose(2, 0, 1, 3).reshape(per_peer, dp_count, feat_cols)
    grad_hidden = jnp.roll(returned, -my_start, axis=1).reshape(slot_rows, feat_cols)
    return (logprobs, grad_hidden)


def solution(mesh):
    return jax.shard_map(
        per_device,
        mesh=mesh,
        in_specs=(P("dp", "vocab"), P(None, ("dp", "vocab")), P(), P("dp"), P("dp"), P("dp")),
        out_specs=(P("dp"), P("dp", "vocab")),
        check_vma=False,
    )
```
